512 devices in a mesh: gx: 8 (over y, core), gy: 4 (over z_hi), gz: 16 (over z_lo, x).
Axes of the slice: x: 4, y: 4, z: 16 (z_hi: 4, z_lo: 4; z = z_hi * 4 + z_lo), core: 2. Of those that a mesh axis runs over, the one named last changes fastest.
Arguments:
- blocks: float32 [8, 4, 16, 8, 128, 128], P('gx', 'gy', 'gz'), as said below
- columns: int32 [8, 4, 16, 8], replicated, may hold values from -1 to 511, as said below
Outputs:
- purified: float32 [8, 4, 16, 8, 128, 128], P('gx', 'gy', 'gz')
The draws below stay inside these ranges and needn't reach their ends.
Inputs may be any that keep to these rules, and one draw needn't show every extreme that they name: columns[i, 0] is i itself; every other entry is -1 or the number of a cluster that differs from i by one along exactly one of the three dimensions, repeats allowed. `blocks`: a block in a slot whose column is -1 is zero.
All inputs are finite; a program needn't handle non-finite values.
Results may differ from the reference program's by a relative error of at most 0.0003.
Values sent between devices are 32-bit elements; how exact they have to be, the bound alone decides.
No kernel may reach another device: no remote copies, remote signals or barrier semaphores. Data moves between devices by JAX's collectives and lax.ppermute only.
A program may use at most 64 MiB of HBM per device.

```python
import math
import jax
import jax.numpy as jnp
from jax import lax

B = 128
K = 8
PURIFY = 1
NX = 8
NY = 4
NZ = 16


def pattern(key):
    clusters = NX * NY * NZ
    cluster_ids = jnp.arange(clusters, dtype=jnp.int32)
    coord_x = cluster_ids // (NY * NZ)
    coord_y = cluster_ids // NZ % NY
    coord_z = cluster_ids % NZ
    heading = jax.random.randint(jax.random.fold_in(key, 11), (clusters, K - 1), 0, 6)
    heading = heading.at[0, 0].set(0)
    step_x = jnp.where(heading == 0, -1, jnp.where(heading == 1, 1, 0))
    step_y = jnp.where(heading == 2, -1, jnp.where(heading == 3, 1, 0))
    step_z = jnp.where(heading == 4, -1, jnp.where(heading == 5, 1, 0))
    near_x = coord_x[:, None] + step_x
    near_y = coord_y[:, None] + step_y
    near_z = coord_z[:, None] + step_z
    inside = (near_x >= 0) & (near_x < NX) & (near_y >= 0) & (near_y < NY) & (near_z >= 0) & (near_z < NZ)
    others = jnp.where(inside, (near_x * NY + near_y) * NZ + near_z, -1)
    joined = jnp.concatenate([cluster_ids[:, None], others], axis=1)
    return joined.astype(jnp.int32).reshape(NX, NY, NZ, K)


def draw_columns(key, part):
    return pattern(jax.random.fold_in(key, 5))


def draw_blocks(key, part):
    pattern_cols = pattern(jax.random.fold_in(key, 5))
    sigma = 0.45 / math.sqrt(K * B)
    shape_all = (NX, NY, NZ, K, B, B)
    noise = jax.random.normal(jax.random.fold_in(key, 21), shape_all, jnp.float32)
    diag_vals = jax.random.uniform(jax.random.fold_in(key, 22), (NX, NY, NZ, B), jnp.float32, 0.2, 0.8)
    values = noise * sigma
    identity = jnp.eye(B, dtype=jnp.float32)
    first_slot = (jnp.arange(K) == 0).astype(jnp.float32)[:, None, None]
    values = values + first_slot * (diag_vals[:, :, :, None, None, :] * identity)
    live = (pattern_cols >= 0)[..., None, None]
    return jnp.where(live, values, 0.0).astype(jnp.float32)


def setup_inputs(seed: int = 0) -> dict:
    keys = jax.random.split(jax.random.key(seed), 3)
    return {
        "blocks": draw_blocks(jax.random.fold_in(keys[2], 71), 0),
        "columns": draw_columns(jax.random.fold_in(keys[2], 71), 0),
    }


exact_mode = lax.Precision.HIGHEST


def purify_once(current, flat_cols):
    flat_blocks = current.reshape(-1, K, B, B)

    def one_row(packed):
        row_blocks, row_cols = packed
        safe_cols = jnp.maximum(row_cols, 0)
        far_rows = flat_blocks[safe_cols]
        far_cols = flat_cols[safe_cols]
        matches = (far_cols[:, :, None] == row_cols[None, None, :]) & (row_cols[None, None, :] >= 0) & (row_cols[:, None, None] >= 0)
        picked = jnp.einsum("tus,tuab->tsab", matches.astype(jnp.float32), far_rows, precision=exact_mode)
        square = jnp.einsum("tab,tsbc->sac", row_blocks, picked, precision=exact_mode)
        cubed = jnp.einsum("tab,tsbc->sac", square, picked, precision=exact_mode)
        return 3.0 * square - 2.0 * cubed

    return lax.map(one_row, (flat_blocks, flat_cols)).reshape(current.shape)


def reference(blocks, columns):
    flat_cols = columns.reshape(-1, K)
    current = blocks
    for sweep in range(PURIFY):
        current = purify_once(current, flat_cols)
    return current
```

```python
import functools

import jax
import jax.numpy as jnp
from jax import lax
from jax.experimental import pallas as pl
from jax.experimental.pallas import tpu as pltpu
from jax.sharding import PartitionSpec as P

SIDES = (("gy", 1), ("gy", -1), ("gx", 1), ("gx", -1), ("gz", 1), ("gz", -1))


VMEM_BYTES = 8 * 1024 * 1024


def place(columns_shape):
    _, total_y, _, total_z = columns_shape
    x, y, z = lax.axis_index("gx"), lax.axis_index("gy"), lax.axis_index("gz")
    return (x * total_y + y) * total_z + z, x, y, z


def strides(columns_shape):
    _, total_y, _, total_z = columns_shape
    size = {"gx": total_y * total_z, "gy": total_z, "gz": 1}
    return tuple(step * size[axis] for axis, step in SIDES)


def outgoing(steps, columns, blocks, *rest):
    sends, (rows, sem) = rest[: len(steps)], rest[len(steps) :]
    me, x, y, z = place(columns.shape)
    fetch = pltpu.make_async_copy(columns.at[x, y], rows, sem)
    fetch.start()
    fetch.wait()
    kslots, size = blocks.shape[3], blocks.shape[4]
    weights = []
    for step in steps:
        column = me + step
        weights.append(
            [jnp.where(rows[s, z] == column, 1.0, 0.0).astype(jnp.float32) for s in range(1, kslots)]
        )
    for start in range(0, size, 8):
        part = pl.ds(start, 8)
        own = blocks[0, 0, 0, 0, part, :]
        others = [blocks[0, 0, 0, s, part, :] for s in range(1, kslots)]
        for send, weight in zip(sends, weights):
            send[0, part, :] = own
            send[1, part, :] = sum(w * v for w, v in zip(weight, others))


def halves(value):
    high = value.astype(jnp.bfloat16)
    return high, (value - high.astype(jnp.float32)).astype(jnp.bfloat16)


def left(value):
    high, low = halves(value)
    return jnp.concatenate([high, low, high], axis=1)


def right(value):
    high, low = halves(value)
    return jnp.concatenate([high, high, low], axis=0)


def dot(a, b):
    return jnp.dot(a, b, preferred_element_type=jnp.float32)


def finish(steps, columns, *rest):
    count = len(steps)
    sends, gets = rest[:count], rest[count : 2 * count]
    out, results, rows, sem, out_sems = rest[2 * count :]
    me, x, y, z = place(columns.shape)
    fetch = pltpu.make_async_copy(columns.at[x, y], rows, sem)
    fetch.start()
    fetch.wait()
    kslots, size = out.shape[3], out.shape[4]
    named = [rows[s, z] for s in range(kslots)]
    own = sends[0][0]
    row = jnp.concatenate([own] + [send[1] for send in sends], axis=1)
    row = right(row)
    first = dot(left(own), row)
    corner = first[:, :size]
    pairs = [right(jnp.concatenate([get[0], get[1]], axis=1)) for get in gets]
    squares = []
    for d in range(count):
        both = dot(left(sends[d][1]), pairs[d])
        squares.append(first[:, (d + 1) * size : (d + 2) * size] + both[:, :size])
        corner = corner + both[:, size:]
    cubes = dot(left(corner), row)
    cube = cubes[:, :size]
    for d in range(count):
        uses = sum(jnp.where(c == me + steps[d], 1.0, 0.0) for c in named[1:]).astype(jnp.float32)
        both = uses * dot(left(squares[d]), pairs[d])
        cube = cube + both[:, size:]
        far = cubes[:, (d + 1) * size : (d + 2) * size] + both[:, :size]
        results[d + 1] = 3.0 * squares[d] - 2.0 * far
    results[0] = 3.0 * corner - 2.0 * cube
    results[count + 1] = jnp.zeros((size, size), jnp.float32)
    copies = []
    for s in range(kslots):
        source = jnp.int32(count + 1)
        for d, step in enumerate((0,) + steps):
            source = jnp.where((named[s] >= 0) & (named[s] == me + step), d, source)
        copies.append(
            pltpu.make_async_copy(results.at[source], out.at[0, 0, 0, s], out_sems.at[s])
        )
    for copy in copies:
        copy.start()
    for copy in copies:
        copy.wait()


def on_device(blocks, columns):
    kslots, size = blocks.shape[3], blocks.shape[4]
    columns = jnp.swapaxes(columns, 2, 3)
    steps = strides(columns.shape)
    count = len(steps)
    vmem = pl.BlockSpec(memory_space=pltpu.VMEM)
    hbm = pl.BlockSpec(memory_space=pl.ANY)
    pair = jax.ShapeDtypeStruct((2, size, size), jnp.float32)
    rows = pltpu.SMEM(columns.shape[2:], jnp.int32)
    sends = pl.pallas_call(
        functools.partial(outgoing, steps),
        out_shape=(pair,) * count,
        in_specs=[hbm, vmem],
        out_specs=(vmem,) * count,
        scratch_shapes=[rows, pltpu.SemaphoreType.DMA],
        compiler_params=pltpu.CompilerParams(vmem_limit_bytes=VMEM_BYTES),
        name="outgoing",
    )(columns, blocks)
    gets = [None] * count
    for d, (axis, step) in enumerate(SIDES):
        ends = lax.axis_size(axis)
        pairs = [(i, i + step) for i in range(ends) if 0 <= i + step < ends]
        gets[SIDES.index((axis, -step))] = lax.ppermute(sends[d], axis, pairs)
    return pl.pallas_call(
        functools.partial(finish, steps),
        out_shape=jax.ShapeDtypeStruct(blocks.shape, jnp.float32),
        in_specs=[hbm] + [vmem] * (2 * count),
        out_specs=hbm,
        scratch_shapes=[
            pltpu.VMEM((count + 2, size, size), jnp.float32),
            rows,
            pltpu.SemaphoreType.DMA,
            pltpu.SemaphoreType.DMA((kslots,)),
        ],
        compiler_params=pltpu.CompilerParams(vmem_limit_bytes=VMEM_BYTES),
        name="finish",
    )(columns, *sends, *gets)


def solution(mesh):
    return jax.shard_map(
        on_device,
        mesh=mesh,
        in_specs=(P("gx", "gy", "gz", None, None, None), P()),
        out_specs=P("gx", "gy", "gz", None, None, None),
        check_vma=False,
    )
```

```python
import functools

import jax
import jax.numpy as jnp
from jax import lax
from jax.experimental import pallas as pl
from jax.experimental.pallas import tpu as pltpu
from jax.sharding import PartitionSpec as P

SHIFT, SWAP = "shift", "swap"
ROUNDS = (
    ("gz", SWAP, 1),
    ("gy", SHIFT, -1),
    ("gy", SHIFT, 1),
    ("gz", SWAP, 0),
    ("gx", SWAP, 1),
    ("gx", SWAP, 0),
)
VMEM_BYTES = 8 * 1024 * 1024


def moves(round_, count):
    _, kind, which = round_
    if kind == SHIFT:
        return [(i, i + which) for i in range(count) if 0 <= i + which < count]
    firsts = range(which, count - 1, 2)
    return [(i, i + 1) for i in firsts] + [(i + 1, i) for i in firsts]


def place(columns_shape):
    total_x, total_y, _, total_z = columns_shape
    sizes = {"gx": total_x, "gy": total_y, "gz": total_z}
    at = {axis: lax.axis_index(axis) for axis in sizes}
    stride = {"gx": total_y * total_z, "gy": total_z, "gz": 1}
    me = (at["gx"] * total_y + at["gy"]) * total_z + at["gz"]
    partners = []
    for axis, kind, which in ROUNDS:
        step = which
        if kind != SHIFT:
            step = jnp.where(at[axis] % 2 == which, 1, -1)
        there = at[axis] + step
        inside = (there >= 0) & (there < sizes[axis])
        partners.append(jnp.where(inside, me + step * stride[axis], -2))
    return at, me, partners


def bringer(d):
    axis, kind, which = ROUNDS[d]
    return ROUNDS.index((axis, SHIFT, -which)) if kind == SHIFT else d


def fetch_row(columns, rows, sem, at):
    return pltpu.make_async_copy(columns.at[at["gx"], at["gy"]], rows, sem)


def outgoing(parts, columns, blocks, *rest):
    count = len(ROUNDS)
    sends, (uses, held, rows, sem, sems) = rest[:count], rest[count:]
    at, me, partners = place(columns.shape)
    kslots, size = blocks.shape[3], blocks.shape[4]
    height = size // parts
    row = fetch_row(columns, rows, sem, at)
    row.start()
    copies = []
    for n in range(parts):
        part = pl.ds(n * height, height)
        copies.append(
            pltpu.make_async_copy(blocks.at[0, 0, 0, :, part, :], held.at[:, part, :], sems.at[n])
        )
        copies[-1].start()
    row.wait()
    weights = [
        [jnp.where(rows[s, at["gz"]] == partner, 1.0, 0.0).astype(jnp.float32) for s in range(1, kslots)]
        for partner in partners
    ]
    for d, weight in enumerate(weights):
        uses[d] = jnp.full(uses.shape[1:], sum(weight), jnp.float32)
    for n in range(parts):
        copies[n].wait()
        for start in range(n * height, (n + 1) * height, 8):
            part = pl.ds(start, 8)
            own = held[0, part, :]
            others = [held[s, part, :] for s in range(1, kslots)]
            for send, weight in zip(sends, weights):
                send[0, part, :] = own
                send[1, part, :] = sum(w * v for w, v in zip(weight, others))


def halves(value):
    high = value.astype(jnp.bfloat16)
    return high, (value - high.astype(jnp.float32)).astype(jnp.bfloat16)


def left(value):
    high, low = halves(value)
    return jnp.concatenate([high, low, high], axis=1)


def right(value):
    high, low = halves(value)
    return jnp.concatenate([high, high, low], axis=0)


def dot(a, b):
    return jnp.dot(a, b, preferred_element_type=jnp.float32)


def contribute(there, get, straight, uses):
    size = straight.shape[0]
    pair = right(jnp.concatenate([get[0], get[1]], axis=1))
    both = dot(left(there), pair)
    square = straight + both[:, :size]
    twice = dot(left(square), pair)
    return square, both[:, size:], uses * twice[:, :size], uses * twice[:, size:]


def finish(columns, uses, *rest):
    count = len(ROUNDS)
    sends, brought = rest[:count], rest[count : 2 * count]
    out, results, rows, sem, out_sems = rest[2 * count :]
    at, me, partners = place(columns.shape)
    fetch = fetch_row(columns, rows, sem, at)
    fetch.start()
    kslots, size = out.shape[3], out.shape[4]
    own = sends[0][0]
    row = right(jnp.concatenate([own] + [send[1] for send in sends], axis=1))
    first = dot(left(own), row)
    corner = first[:, :size]
    cube = jnp.zeros((size, size), jnp.float32)
    pieces = []
    for d in range(count):
        straight = first[:, (d + 1) * size : (d + 2) * size]
        square, to_corner, far, to_cube = contribute(
            sends[d][1], brought[bringer(d)], straight, uses[d, 0:1, :]
        )
        corner = corner + to_corner
        cube = cube + to_cube
        pieces.append(3.0 * square - 2.0 * far)
    cubes = dot(left(corner), row)
    for d in range(count):
        results[d + 1] = pieces[d] - 2.0 * cubes[:, (d + 1) * size : (d + 2) * size]
    results[0] = 3.0 * corner - 2.0 * (cubes[:, :size] + cube)
    results[count + 1] = jnp.zeros((size, size), jnp.float32)
    fetch.wait()
    copies = []
    for s in range(kslots):
        column = rows[s, at["gz"]]
        source = jnp.int32(count + 1)
        for d, cluster in enumerate([me] + partners):
            source = jnp.where(column == cluster, d, source)
        copies.append(
            pltpu.make_async_copy(results.at[source], out.at[0, 0, 0, s], out_sems.at[s])
        )
    for copy in copies:
        copy.start()
    for copy in copies:
        copy.wait()


def on_device(blocks, columns):
    kslots, size = blocks.shape[3], blocks.shape[4]
    columns = jnp.swapaxes(columns, 2, 3)
    columns = pltpu.with_memory_space_constraint(columns, pltpu.HBM)
    blocks = pltpu.with_memory_space_constraint(blocks, pltpu.HBM)
    count = len(ROUNDS)
    parts = 4
    vmem = pl.BlockSpec(memory_space=pltpu.VMEM)
    hbm = pl.BlockSpec(memory_space=pltpu.HBM)
    params = pltpu.CompilerParams(vmem_limit_bytes=VMEM_BYTES)
    pair = jax.ShapeDtypeStruct((2, size, size), jnp.float32)
    rows = pltpu.SMEM(columns.shape[2:], jnp.int32)
    *sends, uses = pl.pallas_call(
        functools.partial(outgoing, parts),
        out_shape=(pair,) * count + (jax.ShapeDtypeStruct((count, 8, size), jnp.float32),),
        in_specs=[hbm, hbm],
        out_specs=(vmem,) * (count + 1),
        scratch_shapes=[
            pltpu.VMEM((kslots, size, size), jnp.float32),
            rows,
            pltpu.SemaphoreType.DMA,
            pltpu.SemaphoreType.DMA((parts,)),
        ],
        compiler_params=params,
        name="outgoing",
    )(columns, blocks)
    brought = [
        lax.ppermute(send, round_[0], moves(round_, lax.axis_size(round_[0])))
        for round_, send in zip(ROUNDS, sends)
    ]
    return pl.pallas_call(
        finish,
        out_shape=jax.ShapeDtypeStruct(blocks.shape, jnp.float32),
        in_specs=[hbm] + [vmem] * (1 + 2 * count),
        out_specs=hbm,
        scratch_shapes=[
            pltpu.VMEM((count + 2, size, size), jnp.float32),
            rows,
            pltpu.SemaphoreType.DMA,
            pltpu.SemaphoreType.DMA((kslots,)),
        ],
        compiler_params=params,
        name="finish",
    )(columns, uses, *sends, *brought)


def solution(mesh):
    return jax.shard_map(
        on_device,
        mesh=mesh,
        in_specs=(P("gx", "gy", "gz", None, None, None), P()),
        out_specs=P("gx", "gy", "gz", None, None, None),
        check_vma=False,
    )
```

```python
import functools

import jax
import jax.numpy as jnp
from jax import lax
from jax.experimental import pallas as pl
from jax.experimental.pallas import tpu as pltpu
from jax.sharding import PartitionSpec as P

X_EVEN, X_ODD, Y_EVEN, Y_ODD, Z_EVEN, Z_ODD = SWAPS = (
    ("gx", 0),
    ("gx", 1),
    ("gy", 0),
    ("gy", 1),
    ("gz", 0),
    ("gz", 1),
)
AXES = ("gx", "gy", "gz")
ROUNDS = (
    (Y_EVEN, Y_EVEN, None, X_ODD),
    (Z_EVEN, Y_ODD, Y_ODD, None),
    (Z_ODD, Z_ODD, Y_EVEN, Y_EVEN),
    (X_EVEN, Z_EVEN, Z_ODD, Z_ODD),
    (X_ODD, X_ODD, X_ODD, Z_EVEN),
    (None, X_EVEN, Z_EVEN, None),
    (None, None, X_EVEN, X_EVEN),
)
VMEM_BYTES = 8 * 1024 * 1024


def partner_of(at, sizes, swap):
    axis, which = swap
    there = dict(at)
    there[axis] += 1 if at[axis] % 2 == which else -1
    return there if 0 <= there[axis] < sizes[axis] else None


def moves(round_, sizes):
    def index(at):
        return (at["gx"] * sizes["gy"] + at["gy"]) * sizes["gz"] + at["gz"]

    pairs = []
    for x in range(sizes["gx"]):
        for y in range(sizes["gy"]):
            for z in range(sizes["gz"]):
                at = {"gx": x, "gy": y, "gz": z}
                there = round_[y] and partner_of(at, sizes, round_[y])
                if there:
                    pairs.append((index(at), index(there)))
    return pairs


def place(columns_shape):
    total_x, total_y, _, total_z = columns_shape
    sizes = {"gx": total_x, "gy": total_y, "gz": total_z}
    at = {axis: lax.axis_index(axis) for axis in AXES}
    stride = {"gx": total_y * total_z, "gy": total_z, "gz": 1}
    me = (at["gx"] * total_y + at["gy"]) * total_z + at["gz"]
    by_swap = {None: jnp.int32(-2)}
    for axis, which in SWAPS:
        step = jnp.where(at[axis] % 2 == which, 1, -1)
        there = at[axis] + step
        inside = (there >= 0) & (there < sizes[axis])
        by_swap[axis, which] = jnp.where(inside, me + step * stride[axis], -2)
    partners = []
    for round_ in ROUNDS:
        partner = by_swap[round_[0]]
        for y in range(1, total_y):
            if any(round_[y] != round_[0] for y in range(1, total_y)):
                partner = jnp.where(at["gy"] == y, by_swap[round_[y]], partner)
        partners.append(partner)
    return at, me, partners


def fetch_row(columns, rows, sem, at):
    return pltpu.make_async_copy(columns.at[at["gx"], at["gy"]], rows, sem)


def outgoing(parts, columns, blocks, *rest):
    count = len(ROUNDS)
    sends, (uses, held, rows, sem, sems) = rest[:count], rest[count:]
    at, me, partners = place(columns.shape)
    kslots, size = blocks.shape[3], blocks.shape[4]
    height = size // parts
    row = fetch_row(columns, rows, sem, at)
    row.start()
    copies = []
    for n in range(parts):
        part = pl.ds(n * height, height)
        copies.append(
            pltpu.make_async_copy(blocks.at[0, 0, 0, :, part, :], held.at[:, part, :], sems.at[n])
        )
        copies[-1].start()
    row.wait()
    weights = [
        [jnp.where(rows[s, at["gz"]] == partner, 1.0, 0.0).astype(jnp.float32) for s in range(1, kslots)]
        for partner in partners
    ]
    lanes = uses.shape[2]
    for d, weight in enumerate(weights):
        for s, value in enumerate([sum(weight)] + weight):
            uses[d, s : s + 1, :] = jnp.full((1, lanes), value, jnp.float32)
    for n in range(parts):
        copies[n].wait()
        for start in range(n * height, (n + 1) * height, 8):
            part = pl.ds(start, 8)
            own = held[0, part, :]
            others = [held[s, part, :] for s in range(1, kslots)]
            for send, weight in zip(sends, weights):
                send[0, part, :] = own
                send[1, part, :] = sum(w * v for w, v in zip(weight, others))


def halves(value):
    high = value.astype(jnp.bfloat16)
    return high, (value - high.astype(jnp.float32)).astype(jnp.bfloat16)


def left(value):
    high, low = halves(value)
    return jnp.concatenate([high, low, high], axis=1)


def right(value):
    high, low = halves(value)
    return jnp.concatenate([high, high, low], axis=0)


def dot(a, b):
    return jnp.dot(a, b, preferred_element_type=jnp.float32)


def contribute(there, get, straight, uses):
    size = straight.shape[0]
    pair = right(jnp.concatenate([get[0], get[1]], axis=1))
    both = dot(left(there), pair)
    square = straight + both[:, :size]
    twice = dot(left(square), pair)
    return square, both[:, size:], uses * twice[:, :size], uses * twice[:, size:]


def finish(uses, *rest):
    count = len(ROUNDS)
    sends, brought = rest[:count], rest[count : 2 * count]
    out, results, slots, out_sems = rest[2 * count :]
    kslots, size = out.shape[3], out.shape[4]
    own = sends[0][0]
    row = right(jnp.concatenate([own] + [send[1] for send in sends], axis=1))
    first = dot(left(own), row)
    corner = first[:, :size]
    cube = jnp.zeros((size, size), jnp.float32)
    pieces = []
    for d in range(count):
        straight = first[:, (d + 1) * size : (d + 2) * size]
        square, to_corner, far, to_cube = contribute(
            sends[d][1], brought[d], straight, uses[d, 0:1, :]
        )
        corner = corner + to_corner
        cube = cube + to_cube
        pieces.append(3.0 * square - 2.0 * far)
    cubes = dot(left(corner), row)
    copies = [
        pltpu.make_async_copy(slots.at[s], out.at[0, 0, 0, s], out_sems.at[s]) for s in range(kslots)
    ]
    slots[0] = 3.0 * corner - 2.0 * (cubes[:, :size] + cube)
    copies[0].start()
    for d in range(count):
        results[d] = pieces[d] - 2.0 * cubes[:, (d + 1) * size : (d + 2) * size]
    for s in range(1, kslots):
        for start in range(0, size, 8):
            part = pl.ds(start, 8)
            value = jnp.zeros((8, size), jnp.float32)
            for d in range(count):
                value = jnp.where(uses[d, s : s + 1, :] > 0.0, results[d, part, :], value)
            slots[s, part, :] = value
        copies[s].start()
    for copy in copies:
        copy.wait()


def on_device(blocks, columns):
    kslots, size = blocks.shape[3], blocks.shape[4]
    columns = jnp.swapaxes(columns, 2, 3)
    columns = pltpu.with_memory_space_constraint(columns, pltpu.HBM)
    blocks = pltpu.with_memory_space_constraint(blocks, pltpu.HBM)
    count = len(ROUNDS)
    parts = 4
    vmem = pl.BlockSpec(memory_space=pltpu.VMEM)
    hbm = pl.BlockSpec(memory_space=pltpu.HBM)
    params = pltpu.CompilerParams(vmem_limit_bytes=VMEM_BYTES)
    pair = jax.ShapeDtypeStruct((2, size, size), jnp.float32)
    rows = pltpu.SMEM(columns.shape[2:], jnp.int32)
    *sends, uses = pl.pallas_call(
        functools.partial(outgoing, parts),
        out_shape=(pair,) * count + (jax.ShapeDtypeStruct((count, 8, size), jnp.float32),),
        in_specs=[hbm, hbm],
        out_specs=(vmem,) * (count + 1),
        scratch_shapes=[
            pltpu.VMEM((kslots, size, size), jnp.float32),
            rows,
            pltpu.SemaphoreType.DMA,
            pltpu.SemaphoreType.DMA((parts,)),
        ],
        compiler_params=params,
        name="outgoing",
    )(columns, blocks)
    sizes = {axis: lax.axis_size(axis) for axis in AXES}
    brought = [lax.ppermute(send, AXES, moves(round_, sizes)) for round_, send in zip(ROUNDS, sends)]
    return pl.pallas_call(
        finish,
        out_shape=jax.ShapeDtypeStruct(blocks.shape, jnp.float32),
        in_specs=[vmem] * (1 + 2 * count),
        out_specs=hbm,
        scratch_shapes=[
            pltpu.VMEM((count, size, size), jnp.float32),
            pltpu.VMEM((kslots, size, size), jnp.float32),
            pltpu.SemaphoreType.DMA((kslots,)),
        ],
        compiler_params=params,
        name="finish",
    )(uses, *sends, *brought)


def solution(mesh):
    return jax.shard_map(
        on_device,
        mesh=mesh,
        in_specs=(P("gx", "gy", "gz", None, None, None), P()),
        out_specs=P("gx", "gy", "gz", None, None, None),
        check_vma=False,
    )
```

```python
import functools

import jax
import jax.numpy as jnp
import numpy as np
from jax import lax
from jax.experimental import pallas as pl
from jax.experimental.pallas import tpu as pltpu
from jax.sharding import PartitionSpec as P

SCHEDULE = (
    (
        "yXzZx..", "yXzZx..", "yXzZx..", "yZzXx..", "yZzXx..", "yXzZx..", "yXzZx..", "yZzXx..",
        "yZzXx..", "yXzZx..", "yXzZx..", "yZzXx..", "yZzXx..", "yXzZx..", "yXzZx..", "yXzZx..",
    ),
    (
        "yYXzZx.", "yYXzZx.", "yYXzZx.", "yZYzXx.", "yZYzXx.", "yYXzZx.", "yYXzZx.", "yZYzXx.",
        "yZYzXx.", "yYXzZx.", "yYXzZx.", "yZYzXx.", "yZYzXx.", "yYXzZx.", "yYXzZx.", "yYXzZx.",
    ),
    (
        ".YyXZzx", ".YyXZzx", ".YyXZzx", "Z.YyXzx", "Z.YyXzx", ".YyXZzx", ".YyXZzx", "Z.YyXzx",
        "Z.YyXzx", ".YyXZzx", ".YyXZzx", "Z.YyXzx", "Z.YyXzx", ".YyXZzx", ".YyXZzx", ".YyXZzx",
    ),
    (
        "X.yxZz.", "X.yxZz.", "X.yxZz.", "Z..yXzx", "Z..yXzx", "X.yxZz.", "X.yxZz.", "Z..yXzx",
        "Z..yXzx", "X.yxZz.", "X.yxZz.", "Z..yXzx", "Z..yXzx", "X.yxZz.", "X.yxZz.", "X.yxZz.",
    ),
)
ROUNDS = range(len(SCHEDULE[0][0]))
AXES = ("gx", "gy", "gz")
LETTERS = {"x": 0, "y": 1, "z": 2}
EARLY = 2
VMEM_BYTES = 8 * 1024 * 1024


def partners_of(sizes):
    table = np.full((len(ROUNDS),) + sizes, -2, np.int32)
    for at in np.ndindex(sizes):
        for n, letter in enumerate(SCHEDULE[at[1]][at[2]]):
            if letter == ".":
                continue
            axis = LETTERS[letter.lower()]
            there = list(at)
            there[axis] += 1 if at[axis] % 2 == letter.isupper() else -1
            if 0 <= there[axis] < sizes[axis]:
                table[(n,) + at] = np.ravel_multi_index(there, sizes)
    return table


def fetch_row(table, rows, sem):
    place = table.at[lax.axis_index("gx"), lax.axis_index("gy")]
    return pltpu.make_async_copy(place, rows, sem)


def outgoing(parts, columns, partners, blocks, *rest):
    count = len(ROUNDS)
    sends, (uses, held, rows, near, row_sems, sems) = rest[:count], rest[count:]
    kslots, size = blocks.shape[3], blocks.shape[4]
    height = size // parts
    fetches = [
        fetch_row(columns, rows, row_sems.at[0]),
        fetch_row(partners, near, row_sems.at[1]),
    ]
    for fetch in fetches:
        fetch.start()
    copies = []
    for n in range(parts):
        part = pl.ds(n * height, height)
        copies.append(
            pltpu.make_async_copy(blocks.at[0, 0, 0, :, part, :], held.at[:, part, :], sems.at[n])
        )
        copies[-1].start()
    for fetch in fetches:
        fetch.wait()
    z = lax.axis_index("gz")
    named = [rows[s, z] for s in range(1, kslots)]
    weights = [
        [jnp.where(column == near[n, z], 1.0, 0.0).astype(jnp.float32) for column in named]
        for n in ROUNDS
    ]
    lanes = uses.shape[2]
    for d, weight in enumerate(weights):
        for s, value in enumerate([sum(weight)] + weight):
            uses[d, s : s + 1, :] = jnp.full((1, lanes), value, jnp.float32)
    for n in range(parts):
        copies[n].wait()
        for start in range(n * height, (n + 1) * height, 8):
            part = pl.ds(start, 8)
            own = held[0, part, :]
            others = [held[s, part, :] for s in range(1, kslots)]
            for send, weight in zip(sends, weights):
                send[0, part, :] = own
                send[1, part, :] = sum(w * v for w, v in zip(weight, others))


def halves(value):
    high = value.astype(jnp.bfloat16)
    return high, (value - high.astype(jnp.float32)).astype(jnp.bfloat16)


def left(value):
    high, low = halves(value)
    return jnp.concatenate([high, low, high], axis=1)


def right(value):
    high, low = halves(value)
    return jnp.concatenate([high, high, low], axis=0)


def dot(a, b):
    return jnp.dot(a, b, preferred_element_type=jnp.float32)


def contribute(there, get, straight, uses):
    size = straight.shape[0]
    pair = right(jnp.concatenate([get[0], get[1]], axis=1))
    both = dot(left(there), pair)
    square = straight + both[:, :size]
    twice = dot(left(square), pair)
    return square, both[:, size:], uses * twice[:, :size], uses * twice[:, size:]


def early(uses, *rest):
    count = len(ROUNDS)
    sends, brought = rest[:count], rest[count : count + EARLY]
    partial, row_out = rest[count + EARLY :]
    size = partial.shape[1]
    own = sends[0][0]
    row = right(jnp.concatenate([own] + [send[1] for send in sends], axis=1))
    row_out[...] = row
    first = dot(left(own), row)
    corner = first[:, :size]
    cube = jnp.zeros((size, size), jnp.float32)
    for d in range(count):
        straight = first[:, (d + 1) * size : (d + 2) * size]
        if d < EARLY:
            square, to_corner, far, to_cube = contribute(
                sends[d][1], brought[d], straight, uses[d, 0:1, :]
            )
            corner = corner + to_corner
            cube = cube + to_cube
            straight = 3.0 * square - 2.0 * far
        partial[d] = straight
    partial[count] = corner
    partial[count + 1] = cube


def finish(uses, partial, row_in, *rest):
    count = len(ROUNDS)
    late = count - EARLY
    sends, brought = rest[:late], rest[late : 2 * late]
    out, results, slots, out_sems = rest[2 * late :]
    kslots, size = out.shape[3], out.shape[4]
    corner = partial[count]
    cube = partial[count + 1]
    pieces = [partial[d] for d in range(count)]
    for d in range(EARLY, count):
        square, to_corner, far, to_cube = contribute(
            sends[d - EARLY][1], brought[d - EARLY], pieces[d], uses[d, 0:1, :]
        )
        corner = corner + to_corner
        cube = cube + to_cube
        pieces[d] = 3.0 * square - 2.0 * far
    cubes = dot(left(corner), row_in[...])
    copies = [
        pltpu.make_async_copy(slots.at[s], out.at[0, 0, 0, s], out_sems.at[s]) for s in range(kslots)
    ]
    slots[0] = 3.0 * corner - 2.0 * (cubes[:, :size] + cube)
    copies[0].start()
    for d in range(count):
        results[d] = pieces[d] - 2.0 * cubes[:, (d + 1) * size : (d + 2) * size]
    for s in range(1, kslots):
        for start in range(0, size, 8):
            part = pl.ds(start, 8)
            value = jnp.zeros((8, size), jnp.float32)
            for d in range(count):
                value = jnp.where(uses[d, s : s + 1, :] > 0.0, results[d, part, :], value)
            slots[s, part, :] = value
        copies[s].start()
    for copy in copies:
        copy.wait()


def on_device(blocks, columns):
    kslots, size = blocks.shape[3], blocks.shape[4]
    columns = jnp.swapaxes(columns, 2, 3)
    sizes = tuple(lax.axis_size(axis) for axis in AXES)
    table = partners_of(sizes)
    partners = jnp.asarray(table.transpose(1, 2, 0, 3))
    columns = pltpu.with_memory_space_constraint(columns, pltpu.HBM)
    partners = pltpu.with_memory_space_constraint(partners, pltpu.HBM)
    blocks = pltpu.with_memory_space_constraint(blocks, pltpu.HBM)
    count = len(ROUNDS)
    parts = 4
    vmem = pl.BlockSpec(memory_space=pltpu.VMEM)
    hbm = pl.BlockSpec(memory_space=pltpu.HBM)
    params = pltpu.CompilerParams(vmem_limit_bytes=VMEM_BYTES)
    pair = jax.ShapeDtypeStruct((2, size, size), jnp.float32)
    *sends, uses = pl.pallas_call(
        functools.partial(outgoing, parts),
        out_shape=(pair,) * count + (jax.ShapeDtypeStruct((count, 8, size), jnp.float32),),
        in_specs=[hbm, hbm, hbm],
        out_specs=(vmem,) * (count + 1),
        scratch_shapes=[
            pltpu.VMEM((kslots, size, size), jnp.float32),
            pltpu.SMEM(columns.shape[2:], jnp.int32),
            pltpu.SMEM(partners.shape[2:], jnp.int32),
            pltpu.SemaphoreType.DMA((2,)),
            pltpu.SemaphoreType.DMA((parts,)),
        ],
        compiler_params=params,
        name="outgoing",
    )(columns, partners, blocks)
    brought = [
        lax.ppermute(send, AXES, [(i, int(j)) for i, j in enumerate(row.ravel()) if j >= 0])
        for row, send in zip(table, sends)
    ]
    partial, row = pl.pallas_call(
        early,
        out_shape=(
            jax.ShapeDtypeStruct((count + 2, size, size), jnp.float32),
            jax.ShapeDtypeStruct((3 * size, (count + 1) * size), jnp.bfloat16),
        ),
        in_specs=[vmem] * (1 + count + EARLY),
        out_specs=(vmem, vmem),
        compiler_params=params,
        name="early",
    )(uses, *sends, *brought[:EARLY])
    return pl.pallas_call(
        finish,
        out_shape=jax.ShapeDtypeStruct(blocks.shape, jnp.float32),
        in_specs=[vmem] * (3 + 2 * (count - EARLY)),
        out_specs=hbm,
        scratch_shapes=[
            pltpu.VMEM((count, size, size), jnp.float32),
            pltpu.VMEM((kslots, size, size), jnp.float32),
            pltpu.SemaphoreType.DMA((kslots,)),
        ],
        compiler_params=params,
        name="finish",
    )(uses, partial, row, *sends[EARLY:], *brought[EARLY:])


def solution(mesh):
    return jax.shard_map(
        on_device,
        mesh=mesh,
        in_specs=(P("gx", "gy", "gz", None, None, None), P()),
        out_specs=P("gx", "gy", "gz", None, None, None),
        check_vma=False,
    )
```

```python
import functools

import jax
import jax.numpy as jnp
import numpy as np
from jax import lax
from jax.experimental import pallas as pl
from jax.experimental.pallas import tpu as pltpu
from jax.sharding import PartitionSpec as P

SCHEDULE = (
    (
        "yXzZx..", "yXzZx..", "yXzZx..", "yZzXx..", "yZzXx..", "yXzZx..", "yXzZx..", "yZzXx..",
        "yZzXx..", "yXzZx..", "yXzZx..", "yZzXx..", "yZzXx..", "yXzZx..", "yXzZx..", "yXzZx..",
    ),
    (
        "yYXzZx.", "yYXzZx.", "yYXzZx.", "yZYzXx.", "yZYzXx.", "yYXzZx.", "yYXzZx.", "yZYzXx.",
        "yZYzXx.", "yYXzZx.", "yYXzZx.", "yZYzXx.", "yZYzXx.", "yYXzZx.", "yYXzZx.", "yYXzZx.",
    ),
    (
        ".YyXZzx", ".YyXZzx", ".YyXZzx", "Z.YyXzx", "Z.YyXzx", ".YyXZzx", ".YyXZzx", "Z.YyXzx",
        "Z.YyXzx", ".YyXZzx", ".YyXZzx", "Z.YyXzx", "Z.YyXzx", ".YyXZzx", ".YyXZzx", ".YyXZzx",
    ),
    (
        "X.yxZz.", "X.yxZz.", "X.yxZz.", "Z..yXzx", "Z..yXzx", "X.yxZz.", "X.yxZz.", "Z..yXzx",
        "Z..yXzx", "X.yxZz.", "X.yxZz.", "Z..yXzx", "Z..yXzx", "X.yxZz.", "X.yxZz.", "X.yxZz.",
    ),
)
ROUNDS = range(len(SCHEDULE[0][0]))
AXES = ("gx", "gy", "gz")
LETTERS = {"x": 0, "y": 1, "z": 2}
EARLY = 2
VMEM_BYTES = 8 * 1024 * 1024


def partners_of(sizes):
    table = np.full((len(ROUNDS),) + sizes, -2, np.int32)
    for at in np.ndindex(sizes):
        for n, letter in enumerate(SCHEDULE[at[1]][at[2]]):
            if letter == ".":
                continue
            axis = LETTERS[letter.lower()]
            there = list(at)
            there[axis] += 1 if at[axis] % 2 == letter.isupper() else -1
            if 0 <= there[axis] < sizes[axis]:
                table[(n,) + at] = np.ravel_multi_index(there, sizes)
    return table


def fetch_row(table, rows, sem):
    place = table.at[lax.axis_index("gx"), lax.axis_index("gy")]
    return pltpu.make_async_copy(place, rows, sem)


def outgoing(parts, columns, partners, blocks, *rest):
    count = len(ROUNDS)
    sends, (uses, held, rows, near, row_sems, sems) = rest[:count], rest[count:]
    kslots, size = blocks.shape[3], blocks.shape[4]
    height = size // parts
    fetches = [
        fetch_row(columns, rows, row_sems.at[0]),
        fetch_row(partners, near, row_sems.at[1]),
    ]
    for fetch in fetches:
        fetch.start()
    copies = []
    for n in range(parts):
        part = pl.ds(n * height, height)
        copies.append(
            pltpu.make_async_copy(blocks.at[0, 0, 0, :, part, :], held.at[:, part, :], sems.at[n])
        )
        copies[-1].start()
    for fetch in fetches:
        fetch.wait()
    z = lax.axis_index("gz")
    named = [rows[s, z] for s in range(1, kslots)]
    weights = [
        [jnp.where(column == near[n, z], 1.0, 0.0).astype(jnp.float32) for column in named]
        for n in ROUNDS
    ]
    lanes = uses.shape[2]
    for d, weight in enumerate(weights):
        for s, value in enumerate([sum(weight)] + weight):
            uses[d, s : s + 1, :] = jnp.full((1, lanes), value, jnp.float32)
    for n in range(parts):
        copies[n].wait()
        for start in range(n * height, (n + 1) * height, 8):
            part = pl.ds(start, 8)
            own = held[0, part, :]
            others = [held[s, part, :] for s in range(1, kslots)]
            for send, weight in zip(sends, weights):
                send[0, part, :] = own
                send[1, part, :] = sum(w * v for w, v in zip(weight, others))


def halves(value):
    high = value.astype(jnp.bfloat16)
    return high, (value - high.astype(jnp.float32)).astype(jnp.bfloat16)


def left(value):
    high, low = halves(value)
    return jnp.concatenate([high, low, high], axis=1)


def right(value):
    high, low = halves(value)
    return jnp.concatenate([high, high, low], axis=0)


def dot(a, b):
    return jnp.dot(a, b, preferred_element_type=jnp.float32)


def contribute(there, get, straight, uses):
    size = straight.shape[0]
    pair = right(jnp.concatenate([get[0], get[1]], axis=1))
    both = dot(left(there), pair)
    square = straight + both[:, :size]
    twice = dot(left(square), pair)
    return square, both[:, size:], uses * twice[:, :size], uses * twice[:, size:]


def early(uses, *rest):
    count = len(ROUNDS)
    sends, brought = rest[:count], rest[count : count + EARLY]
    partial, row_out = rest[count + EARLY :]
    size = partial.shape[1]
    own = sends[0][0]
    row = right(jnp.concatenate([own] + [send[1] for send in sends], axis=1))
    row_out[...] = row
    first = dot(left(own), row)
    corner = first[:, :size]
    cube = jnp.zeros((size, size), jnp.float32)
    for d in range(count):
        straight = first[:, (d + 1) * size : (d + 2) * size]
        if d < EARLY:
            square, to_corner, far, to_cube = contribute(
                sends[d][1], brought[d], straight, uses[d, 0:1, :]
            )
            corner = corner + to_corner
            cube = cube + to_cube
            straight = 3.0 * square - 2.0 * far
        partial[d] = straight
    partial[count] = corner
    partial[count + 1] = cube


def finish(uses, partial, row_in, *rest):
    count = len(ROUNDS)
    late = count - EARLY
    sends, brought = rest[:late], rest[late : 2 * late]
    out, results, slots, out_sems = rest[2 * late :]
    kslots, size = out.shape[3], out.shape[4]
    corner = partial[count]
    cube = partial[count + 1]
    pieces = [partial[d] for d in range(count)]
    for d in range(EARLY, count):
        square, to_corner, far, to_cube = contribute(
            sends[d - EARLY][1], brought[d - EARLY], pieces[d], uses[d, 0:1, :]
        )
        corner = corner + to_corner
        cube = cube + to_cube
        pieces[d] = 3.0 * square - 2.0 * far
    cubes = dot(left(corner), row_in[...])
    copies = [
        pltpu.make_async_copy(slots.at[s], out.at[0, 0, 0, s], out_sems.at[s]) for s in range(kslots)
    ]
    slots[0] = 3.0 * corner - 2.0 * (cubes[:, :size] + cube)
    copies[0].start()
    for d in range(count):
        results[d] = pieces[d] - 2.0 * cubes[:, (d + 1) * size : (d + 2) * size]
    for s in range(1, kslots):
        for start in range(0, size, 8):
            part = pl.ds(start, 8)
            value = jnp.zeros((8, size), jnp.float32)
            for d in range(count):
                value = jnp.where(uses[d, s : s + 1, :] > 0.0, results[d, part, :], value)
            slots[s, part, :] = value
        copies[s].start()
    for copy in copies:
        copy.wait()


def on_device(blocks, columns):
    kslots, size = blocks.shape[3], blocks.shape[4]
    columns = jnp.swapaxes(columns, 2, 3)
    sizes = tuple(lax.axis_size(axis) for axis in AXES)
    table = partners_of(sizes)
    partners = jnp.asarray(table.transpose(1, 2, 0, 3))
    columns = pltpu.with_memory_space_constraint(columns, pltpu.HBM)
    partners = pltpu.with_memory_space_constraint(partners, pltpu.HBM)
    blocks = pltpu.with_memory_space_constraint(blocks, pltpu.HBM)
    count = len(ROUNDS)
    parts = 1
    vmem = pl.BlockSpec(memory_space=pltpu.VMEM)
    hbm = pl.BlockSpec(memory_space=pltpu.HBM)
    params = pltpu.CompilerParams(vmem_limit_bytes=VMEM_BYTES)
    pair = jax.ShapeDtypeStruct((2, size, size), jnp.float32)
    *sends, uses = pl.pallas_call(
        functools.partial(outgoing, parts),
        out_shape=(pair,) * count + (jax.ShapeDtypeStruct((count, 8, size), jnp.float32),),
        in_specs=[hbm, hbm, hbm],
        out_specs=(vmem,) * (count + 1),
        scratch_shapes=[
            pltpu.VMEM((kslots, size, size), jnp.float32),
            pltpu.SMEM(columns.shape[2:], jnp.int32),
            pltpu.SMEM(partners.shape[2:], jnp.int32),
            pltpu.SemaphoreType.DMA((2,)),
            pltpu.SemaphoreType.DMA((parts,)),
        ],
        compiler_params=params,
        name="outgoing",
    )(columns, partners, blocks)
    brought = [
        lax.ppermute(send, AXES, [(i, int(j)) for i, j in enumerate(row.ravel()) if j >= 0])
        for row, send in zip(table, sends)
    ]
    partial, row = pl.pallas_call(
        early,
        out_shape=(
            jax.ShapeDtypeStruct((count + 2, size, size), jnp.float32),
            jax.ShapeDtypeStruct((3 * size, (count + 1) * size), jnp.bfloat16),
        ),
        in_specs=[vmem] * (1 + count + EARLY),
        out_specs=(vmem, vmem),
        compiler_params=params,
        name="early",
    )(uses, *sends, *brought[:EARLY])
    return pl.pallas_call(
        finish,
        out_shape=jax.ShapeDtypeStruct(blocks.shape, jnp.float32),
        in_specs=[vmem] * (3 + 2 * (count - EARLY)),
        out_specs=hbm,
        scratch_shapes=[
            pltpu.VMEM((count, size, size), jnp.float32),
            pltpu.VMEM((kslots, size, size), jnp.float32),
            pltpu.SemaphoreType.DMA((kslots,)),
        ],
        compiler_params=params,
        name="finish",
    )(uses, partial, row, *sends[EARLY:], *brought[EARLY:])


def solution(mesh):
    return jax.shard_map(
        on_device,
        mesh=mesh,
        in_specs=(P("gx", "gy", "gz", None, None, None), P()),
        out_specs=P("gx", "gy", "gz", None, None, None),
        check_vma=False,
    )
```

```python
import functools

import jax
import jax.numpy as jnp
import numpy as np
from jax import lax
from jax.experimental import pallas as pl
from jax.experimental.pallas import tpu as pltpu
from jax.sharding import PartitionSpec as P

SCHEDULE = (
    (
        "yXzZx..", "yXzZx..", "yXzZx..", "yZzXx..", "yZzXx..", "yXzZx..", "yXzZx..", "yZzXx..",
        "yZzXx..", "yXzZx..", "yXzZx..", "yZzXx..", "yZzXx..", "yXzZx..", "yXzZx..", "yXzZx..",
    ),
    (
        "yYXzZx.", "yYXzZx.", "yYXzZx.", "yZYzXx.", "yZYzXx.", "yYXzZx.", "yYXzZx.", "yZYzXx.",
        "yZYzXx.", "yYXzZx.", "yYXzZx.", "yZYzXx.", "yZYzXx.", "yYXzZx.", "yYXzZx.", "yYXzZx.",
    ),
    (
        ".YyXZzx", ".YyXZzx", ".YyXZzx", "Z.YyXzx", "Z.YyXzx", ".YyXZzx", ".YyXZzx", "Z.YyXzx",
        "Z.YyXzx", ".YyXZzx", ".YyXZzx", "Z.YyXzx", "Z.YyXzx", ".YyXZzx", ".YyXZzx", ".YyXZzx",
    ),
    (
        "X.yxZz.", "X.yxZz.", "X.yxZz.", "Z..yXzx", "Z..yXzx", "X.yxZz.", "X.yxZz.", "Z..yXzx",
        "Z..yXzx", "X.yxZz.", "X.yxZz.", "Z..yXzx", "Z..yXzx", "X.yxZz.", "X.yxZz.", "X.yxZz.",
    ),
)
ROUNDS = range(len(SCHEDULE[0][0]))
AXES = ("gx", "gy", "gz")
LETTERS = {"x": 0, "y": 1, "z": 2}
EARLY = 2
VMEM_BYTES = 8 * 1024 * 1024


def partners_of(sizes):
    table = np.full((len(ROUNDS),) + sizes, -2, np.int32)
    for at in np.ndindex(sizes):
        for n, letter in enumerate(SCHEDULE[at[1]][at[2]]):
            if letter == ".":
                continue
            axis = LETTERS[letter.lower()]
            there = list(at)
            there[axis] += 1 if at[axis] % 2 == letter.isupper() else -1
            if 0 <= there[axis] < sizes[axis]:
                table[(n,) + at] = np.ravel_multi_index(there, sizes)
    return table


def fetch_row(table, rows, sem):
    place = table.at[lax.axis_index("gx"), lax.axis_index("gy")]
    return pltpu.make_async_copy(place, rows, sem)


def outgoing(parts, columns, partners, blocks, *rest):
    count = len(ROUNDS)
    sends, (uses, held, rows, near, row_sems, sems) = rest[:count], rest[count:]
    kslots, size = blocks.shape[3], blocks.shape[4]
    height = size // parts
    fetches = [
        fetch_row(columns, rows, row_sems.at[0]),
        fetch_row(partners, near, row_sems.at[1]),
    ]
    for fetch in fetches:
        fetch.start()
    copies = []
    for n in range(parts):
        part = pl.ds(n * height, height)
        copies.append(
            pltpu.make_async_copy(blocks.at[0, 0, 0, :, part, :], held.at[:, part, :], sems.at[n])
        )
        copies[-1].start()
    for fetch in fetches:
        fetch.wait()
    z = lax.axis_index("gz")
    named = [rows[s, z] for s in range(1, kslots)]
    weights = [
        [jnp.where(column == near[n, z], 1.0, 0.0).astype(jnp.float32) for column in named]
        for n in ROUNDS
    ]
    lanes = uses.shape[2]
    for d, weight in enumerate(weights):
        for s, value in enumerate([sum(weight)] + weight):
            uses[d, s : s + 1, :] = jnp.full((1, lanes), value, jnp.float32)
    for n in range(parts):
        copies[n].wait()
        for start in range(n * height, (n + 1) * height, 8):
            part = pl.ds(start, 8)
            own = held[0, part, :]
            others = [held[s, part, :] for s in range(1, kslots)]
            for send, weight in zip(sends, weights):
                send[0, part, :] = own
                send[1, part, :] = sum(w * v for w, v in zip(weight, others))


def halves(value):
    high = value.astype(jnp.bfloat16)
    return high, (value - high.astype(jnp.float32)).astype(jnp.bfloat16)


def left(value):
    high, low = halves(value)
    return jnp.concatenate([high, low, high], axis=1)


def right(value):
    high, low = halves(value)
    return jnp.concatenate([high, high, low], axis=0)


def dot(a, b):
    return jnp.dot(a, b, preferred_element_type=jnp.float32)


def contribute(there, get, straight, uses):
    size = straight.shape[0]
    pair = right(jnp.concatenate([get[0], get[1]], axis=1))
    both = dot(left(there), pair)
    square = straight + both[:, :size]
    twice = dot(left(square), pair)
    return square, both[:, size:], uses * twice[:, :size], uses * twice[:, size:]


def early(uses, *rest):
    count = len(ROUNDS)
    sends, brought = rest[:count], rest[count : count + EARLY]
    partial, row_out = rest[count + EARLY :]
    size = partial.shape[1]
    own = sends[0][0]
    row = right(jnp.concatenate([own] + [send[1] for send in sends], axis=1))
    row_out[...] = row
    first = dot(left(own), row)
    corner = first[:, :size]
    cube = jnp.zeros((size, size), jnp.float32)
    for d in range(count):
        straight = first[:, (d + 1) * size : (d + 2) * size]
        if d < EARLY:
            square, to_corner, far, to_cube = contribute(
                sends[d][1], brought[d], straight, uses[d, 0:1, :]
            )
            corner = corner + to_corner
            cube = cube + to_cube
            straight = 3.0 * square - 2.0 * far
        partial[d] = straight
    partial[count] = corner
    partial[count + 1] = cube


def finish(uses, partial, row_in, *rest):
    count = len(ROUNDS)
    late = count - EARLY
    sends, brought = rest[:late], rest[late : 2 * late]
    out, results, slots, out_sems = rest[2 * late :]
    kslots, size = out.shape[3], out.shape[4]
    corner = partial[count]
    cube = partial[count + 1]
    pieces = [partial[d] for d in range(count)]
    for d in range(EARLY, count):
        square, to_corner, far, to_cube = contribute(
            sends[d - EARLY][1], brought[d - EARLY], pieces[d], uses[d, 0:1, :]
        )
        corner = corner + to_corner
        cube = cube + to_cube
        pieces[d] = 3.0 * square - 2.0 * far
    cubes = dot(left(corner), row_in[...])
    copies = [
        pltpu.make_async_copy(slots.at[s], out.at[0, 0, 0, s], out_sems.at[s]) for s in range(kslots)
    ]
    slots[0] = 3.0 * corner - 2.0 * (cubes[:, :size] + cube)
    copies[0].start()
    for d in range(count):
        results[d] = pieces[d] - 2.0 * cubes[:, (d + 1) * size : (d + 2) * size]
    for s in range(1, kslots):
        named = [jnp.broadcast_to(uses[d, s : s + 1, :], (8, size)) > 0.0 for d in range(count)]
        for start in range(0, size, 8):
            part = pl.ds(start, 8)
            value = jnp.zeros((8, size), jnp.float32)
            for d in range(count):
                value = jnp.where(named[d], results[d, part, :], value)
            slots[s, part, :] = value
        copies[s].start()
    for copy in copies:
        copy.wait()


def on_device(blocks, columns):
    kslots, size = blocks.shape[3], blocks.shape[4]
    columns = jnp.swapaxes(columns, 2, 3)
    sizes = tuple(lax.axis_size(axis) for axis in AXES)
    table = partners_of(sizes)
    partners = jnp.asarray(table.transpose(1, 2, 0, 3))
    columns = pltpu.with_memory_space_constraint(columns, pltpu.HBM)
    partners = pltpu.with_memory_space_constraint(partners, pltpu.HBM)
    blocks = pltpu.with_memory_space_constraint(blocks, pltpu.HBM)
    count = len(ROUNDS)
    parts = 4
    vmem = pl.BlockSpec(memory_space=pltpu.VMEM)
    hbm = pl.BlockSpec(memory_space=pltpu.HBM)
    params = pltpu.CompilerParams(vmem_limit_bytes=VMEM_BYTES)
    pair = jax.ShapeDtypeStruct((2, size, size), jnp.float32)
    *sends, uses = pl.pallas_call(
        functools.partial(outgoing, parts),
        out_shape=(pair,) * count + (jax.ShapeDtypeStruct((count, 8, size), jnp.float32),),
        in_specs=[hbm, hbm, hbm],
        out_specs=(vmem,) * (count + 1),
        scratch_shapes=[
            pltpu.VMEM((kslots, size, size), jnp.float32),
            pltpu.SMEM(columns.shape[2:], jnp.int32),
            pltpu.SMEM(partners.shape[2:], jnp.int32),
            pltpu.SemaphoreType.DMA((2,)),
            pltpu.SemaphoreType.DMA((parts,)),
        ],
        compiler_params=params,
        name="outgoing",
    )(columns, partners, blocks)
    brought = [
        lax.ppermute(send, AXES, [(i, int(j)) for i, j in enumerate(row.ravel()) if j >= 0])
        for row, send in zip(table, sends)
    ]
    partial, row = pl.pallas_call(
        early,
        out_shape=(
            jax.ShapeDtypeStruct((count + 2, size, size), jnp.float32),
            jax.ShapeDtypeStruct((3 * size, (count + 1) * size), jnp.bfloat16),
        ),
        in_specs=[vmem] * (1 + count + EARLY),
        out_specs=(vmem, vmem),
        compiler_params=params,
        name="early",
    )(uses, *sends, *brought[:EARLY])
    return pl.pallas_call(
        finish,
        out_shape=jax.ShapeDtypeStruct(blocks.shape, jnp.float32),
        in_specs=[vmem] * (3 + 2 * (count - EARLY)),
        out_specs=hbm,
        scratch_shapes=[
            pltpu.VMEM((count, size, size), jnp.float32),
            pltpu.VMEM((kslots, size, size), jnp.float32),
            pltpu.SemaphoreType.DMA((kslots,)),
        ],
        compiler_params=params,
        name="finish",
    )(uses, partial, row, *sends[EARLY:], *brought[EARLY:])


def solution(mesh):
    return jax.shard_map(
        on_device,
        mesh=mesh,
        in_specs=(P("gx", "gy", "gz", None, None, None), P()),
        out_specs=P("gx", "gy", "gz", None, None, None),
        check_vma=False,
    )
```

```python
import functools

import jax
import jax.numpy as jnp
import numpy as np
from jax import lax
from jax.experimental import pallas as pl
from jax.experimental.pallas import tpu as pltpu
from jax.sharding import PartitionSpec as P

SCHEDULE = (
    (
        "yXzZx..", "yXzZx..", "yXzZx..", "yZzXx..", "yZzXx..", "yXzZx..", "yXzZx..", "yZzXx..",
        "yZzXx..", "yXzZx..", "yXzZx..", "yZzXx..", "yZzXx..", "yXzZx..", "yXzZx..", "yXzZx..",
    ),
    (
        "yYXzZx.", "yYXzZx.", "yYXzZx.", "yZYzXx.", "yZYzXx.", "yYXzZx.", "yYXzZx.", "yZYzXx.",
        "yZYzXx.", "yYXzZx.", "yYXzZx.", "yZYzXx.", "yZYzXx.", "yYXzZx.", "yYXzZx.", "yYXzZx.",
    ),
    (
        ".YyXZzx", ".YyXZzx", ".YyXZzx", "Z.YyXzx", "Z.YyXzx", ".YyXZzx", ".YyXZzx", "Z.YyXzx",
        "Z.YyXzx", ".YyXZzx", ".YyXZzx", "Z.YyXzx", "Z.YyXzx", ".YyXZzx", ".YyXZzx", ".YyXZzx",
    ),
    (
        "X.yxZz.", "X.yxZz.", "X.yxZz.", "Z..yXzx", "Z..yXzx", "X.yxZz.", "X.yxZz.", "Z..yXzx",
        "Z..yXzx", "X.yxZz.", "X.yxZz.", "Z..yXzx", "Z..yXzx", "X.yxZz.", "X.yxZz.", "X.yxZz.",
    ),
)
ROUNDS = range(len(SCHEDULE[0][0]))
AXES = ("gx", "gy", "gz")
LETTERS = {"x": 0, "y": 1, "z": 2}
EARLY = 2
VMEM_BYTES = 8 * 1024 * 1024


def partners_of(sizes):
    table = np.full((len(ROUNDS),) + sizes, -2, np.int32)
    for at in np.ndindex(sizes):
        for n, letter in enumerate(SCHEDULE[at[1]][at[2]]):
            if letter == ".":
                continue
            axis = LETTERS[letter.lower()]
            there = list(at)
            there[axis] += 1 if at[axis] % 2 == letter.isupper() else -1
            if 0 <= there[axis] < sizes[axis]:
                table[(n,) + at] = np.ravel_multi_index(there, sizes)
    return table


def fetch_row(table, rows, sem):
    place = table.at[lax.axis_index("gx"), lax.axis_index("gy")]
    return pltpu.make_async_copy(place, rows, sem)


def outgoing(parts, columns, partners, blocks, *rest):
    count = len(ROUNDS)
    sends, (uses, held, rows, near, row_sems, sems) = rest[:count], rest[count:]
    kslots, size = blocks.shape[3], blocks.shape[4]
    height = size // parts
    fetches = [
        fetch_row(columns, rows, row_sems.at[0]),
        fetch_row(partners, near, row_sems.at[1]),
    ]
    for fetch in fetches:
        fetch.start()
    copies = []
    for n in range(parts):
        part = pl.ds(n * height, height)
        copies.append(
            pltpu.make_async_copy(blocks.at[0, 0, 0, :, part, :], held.at[:, part, :], sems.at[n])
        )
        copies[-1].start()
    for fetch in fetches:
        fetch.wait()
    z = lax.axis_index("gz")
    named = [rows[s, z] for s in range(1, kslots)]
    weights = [
        [jnp.where(column == near[n, z], 1.0, 0.0).astype(jnp.float32) for column in named]
        for n in ROUNDS
    ]
    lanes = uses.shape[2]
    for d, weight in enumerate(weights):
        for s, value in enumerate([sum(weight)] + weight):
            uses[d, s : s + 1, :] = jnp.full((1, lanes), value, jnp.float32)
    for n in range(parts):
        copies[n].wait()
        for start in range(n * height, (n + 1) * height, 8):
            part = pl.ds(start, 8)
            own = held[0, part, :]
            others = [held[s, part, :] for s in range(1, kslots)]
            for send, weight in zip(sends, weights):
                send[0, part, :] = own
                send[1, part, :] = sum(w * v for w, v in zip(weight, others))


def halves(value):
    high = value.astype(jnp.bfloat16)
    return high, (value - high.astype(jnp.float32)).astype(jnp.bfloat16)


def left(value):
    high, low = halves(value)
    return jnp.concatenate([high, low, high], axis=1)


def right(value):
    high, low = halves(value)
    return jnp.concatenate([high, high, low], axis=0)


def dot(a, b):
    return jnp.dot(a, b, preferred_element_type=jnp.float32)


def contribute(there, get, straight, uses):
    size = straight.shape[0]
    pair = right(jnp.concatenate([get[0], get[1]], axis=1))
    both = dot(left(there), pair)
    square = straight + both[:, :size]
    twice = dot(left(square), pair)
    return square, both[:, size:], uses * twice[:, :size], uses * twice[:, size:]


def early(uses, *rest):
    count = len(ROUNDS)
    sends, brought = rest[:count], rest[count : count + EARLY]
    partial, row_out = rest[count + EARLY :]
    size = partial.shape[1]
    own = sends[0][0]
    row = right(jnp.concatenate([own] + [send[1] for send in sends], axis=1))
    row_out[...] = row
    first = dot(left(own), row)
    corner = first[:, :size]
    cube = jnp.zeros((size, size), jnp.float32)
    for d in range(count):
        straight = first[:, (d + 1) * size : (d + 2) * size]
        if d < EARLY:
            square, to_corner, far, to_cube = contribute(
                sends[d][1], brought[d], straight, uses[d, 0:1, :]
            )
            corner = corner + to_corner
            cube = cube + to_cube
            straight = 3.0 * square - 2.0 * far
        partial[d] = straight
    partial[count] = corner
    partial[count + 1] = cube


def finish(uses, partial, row_in, *rest):
    count = len(ROUNDS)
    late = count - EARLY
    sends, brought = rest[:late], rest[late : 2 * late]
    out, results, slots, out_sems = rest[2 * late :]
    kslots, size = out.shape[3], out.shape[4]
    corner = partial[count]
    cube = partial[count + 1]
    pieces = [partial[d] for d in range(count)]
    for d in range(EARLY, count):
        square, to_corner, far, to_cube = contribute(
            sends[d - EARLY][1], brought[d - EARLY], pieces[d], uses[d, 0:1, :]
        )
        corner = corner + to_corner
        cube = cube + to_cube
        pieces[d] = 3.0 * square - 2.0 * far
    cubes = dot(left(corner), row_in[...])
    copies = [
        pltpu.make_async_copy(slots.at[s], out.at[0, 0, 0, s], out_sems.at[s]) for s in range(kslots)
    ]
    slots[0] = 3.0 * corner - 2.0 * (cubes[:, :size] + cube)
    copies[0].start()
    for d in range(count):
        results[d] = pieces[d] - 2.0 * cubes[:, (d + 1) * size : (d + 2) * size]
    for s in range(1, kslots):
        named = [jnp.broadcast_to(uses[d, s : s + 1, :], (8, size)) > 0.0 for d in range(count)]
        for start in range(0, size, 8):
            part = pl.ds(start, 8)
            value = jnp.zeros((8, size), jnp.float32)
            for d in range(count):
                value = jnp.where(named[d], results[d, part, :], value)
            slots[s, part, :] = value
        copies[s].start()
    for copy in copies:
        copy.wait()


def on_device(blocks, columns):
    kslots, size = blocks.shape[3], blocks.shape[4]
    columns = jnp.swapaxes(columns, 2, 3)
    sizes = tuple(lax.axis_size(axis) for axis in AXES)
    table = partners_of(sizes)
    partners = jnp.asarray(table.transpose(1, 2, 0, 3))
    columns = pltpu.with_memory_space_constraint(columns, pltpu.HBM)
    partners = pltpu.with_memory_space_constraint(partners, pltpu.HBM)
    blocks = pltpu.with_memory_space_constraint(blocks, pltpu.HBM)
    count = len(ROUNDS)
    parts = 2
    vmem = pl.BlockSpec(memory_space=pltpu.VMEM)
    hbm = pl.BlockSpec(memory_space=pltpu.HBM)
    params = pltpu.CompilerParams(vmem_limit_bytes=VMEM_BYTES)
    pair = jax.ShapeDtypeStruct((2, size, size), jnp.float32)
    *sends, uses = pl.pallas_call(
        functools.partial(outgoing, parts),
        out_shape=(pair,) * count + (jax.ShapeDtypeStruct((count, 8, size), jnp.float32),),
        in_specs=[hbm, hbm, hbm],
        out_specs=(vmem,) * (count + 1),
        scratch_shapes=[
            pltpu.VMEM((kslots, size, size), jnp.float32),
            pltpu.SMEM(columns.shape[2:], jnp.int32),
            pltpu.SMEM(partners.shape[2:], jnp.int32),
            pltpu.SemaphoreType.DMA((2,)),
            pltpu.SemaphoreType.DMA((parts,)),
        ],
        compiler_params=params,
        name="outgoing",
    )(columns, partners, blocks)
    brought = [
        lax.ppermute(send, AXES, [(i, int(j)) for i, j in enumerate(row.ravel()) if j >= 0])
        for row, send in zip(table, sends)
    ]
    partial, row = pl.pallas_call(
        early,
        out_shape=(
            jax.ShapeDtypeStruct((count + 2, size, size), jnp.float32),
            jax.ShapeDtypeStruct((3 * size, (count + 1) * size), jnp.bfloat16),
        ),
        in_specs=[vmem] * (1 + count + EARLY),
        out_specs=(vmem, vmem),
        compiler_params=params,
        name="early",
    )(uses, *sends, *brought[:EARLY])
    return pl.pallas_call(
        finish,
        out_shape=jax.ShapeDtypeStruct(blocks.shape, jnp.float32),
        in_specs=[vmem] * (3 + 2 * (count - EARLY)),
        out_specs=hbm,
        scratch_shapes=[
            pltpu.VMEM((count, size, size), jnp.float32),
            pltpu.VMEM((kslots, size, size), jnp.float32),
            pltpu.SemaphoreType.DMA((kslots,)),
        ],
        compiler_params=params,
        name="finish",
    )(uses, partial, row, *sends[EARLY:], *brought[EARLY:])


def solution(mesh):
    return jax.shard_map(
        on_device,
        mesh=mesh,
        in_specs=(P("gx", "gy", "gz", None, None, None), P()),
        out_specs=P("gx", "gy", "gz", None, None, None),
        check_vma=False,
    )
```
